128 devices in a mesh: row: 16 (over x, y_lo, core), col: 8 (over y_hi, z).
Axes of the slice: x: 4, y: 4 (y_hi: 2, y_lo: 2; y = y_hi * 2 + y_lo), z: 4, core: 2. Of those that a mesh axis runs over, the one named last changes fastest.
Arguments:
- blocks: bfloat16 [1024, 64, 128, 128], P('row', 'col'), may hold values from -0.109375 to 0.109375
- columns: int32 [1024, 64], P('row', 'col'), may hold values from 0 to 127
- counts: int32 [1024, 8], P('row', 'col'), may hold values from 1 to 8, as said below
- vectors: bfloat16 [1024, 32, 128], P(('col', 'row')), may hold values from -6 to 6
Outputs:
- first_image: bfloat16 [1024, 32, 128], P(('row', 'col'))
- first_back: bfloat16 [1024, 32, 128], P(('col', 'row'))
- second_image: bfloat16 [1024, 32, 128], P(('row', 'col'))
- second_back: bfloat16 [1024, 32, 128], P(('col', 'row'))
The draws below stay inside these ranges and needn't reach their ends.
Inputs may be any that keep to these rules, and one draw needn't show every extreme that they name: `counts`: the live slots are the leading ones; the largest count, 8, is reached in every draw.
All inputs are finite; a program needn't handle non-finite values.
Results may differ from the reference program's by a relative error of at most 0.022.
Values may be sent and summed in bfloat16 or wider, within the bound.
A program may use at most 64 MiB of HBM per device.

```python
import jax
import jax.numpy as jnp
from jax import lax

BS = 128
K = 32
NNZ = 8
VB = 8
NB = 1024
RB = 64
CB = 128
N_ROW = 16
N_COL = 8


def draw_counts(key, part):
    key = jax.random.fold_in(key, 5)
    key_levels, key_rows, key_spot = jax.random.split(key, 3)
    row_groups = NB // RB
    col_groups = RB // VB
    shifts = jax.random.randint(key_levels, (row_groups, col_groups), 0, 3)
    levels = jnp.right_shift(jnp.full((row_groups, col_groups), NNZ, jnp.int32), shifts)
    spot = jax.random.randint(key_spot, (), 0, row_groups * col_groups)
    places = jnp.arange(row_groups * col_groups, dtype=jnp.int32).reshape(row_groups, col_groups)
    levels = jnp.where(places == spot, NNZ, levels)
    levels = jnp.maximum(levels, 1)
    row_levels = jnp.repeat(levels, RB, axis=0)
    drawn = jax.random.randint(key_rows, (NB, col_groups), 1, row_levels + 1)
    last_rows = (jnp.arange(NB, dtype=jnp.int32) % RB == RB - 1)[:, None]
    return jnp.where(last_rows, row_levels, drawn).astype(jnp.int32)


def set_ends(values, own_key, smallest, high):
    longest = values.shape.index(max(values.shape))
    spots = []
    for shift in (0, 1):
        where = [jax.random.randint(jax.random.fold_in(own_key, axis), (), 0, length) for axis, length in enumerate(values.shape)]
        where[longest] = (where[longest] + shift) % values.shape[longest]
        spots.append(tuple(where))
    return values.at[spots[0]].set(smallest).at[spots[1]].set(high)


def block_levels(own_key, extent, cuts, smallest, high):
    level, own = 1.0, jax.random.fold_in(own_key, 6)
    for position, shards_of in cuts:
        steps = jnp.exp(jax.random.uniform(jax.random.fold_in(own, position), (shards_of,), jnp.float32, smallest / len(cuts), high / len(cuts)))
        level = level * jnp.repeat(steps, extent[position] // shards_of).reshape([-1 if axis == position else 1 for axis in range(len(extent))])
    return level


def bell_draw(key, dims, spread, reach, cuts=(), kind=jnp.bfloat16):
    entries = jax.random.normal(key, dims, jnp.float32) * spread
    if len(cuts) > 0:
        entries = block_levels(key, dims, cuts, -0.22, 0.18) * entries
    return jnp.clip(entries, min=-reach, max=reach).astype(kind)


def setup_inputs(seed: int = 0) -> dict:
    key_list = jax.random.split(jax.random.key(seed), 5)
    blocks = bell_draw(key_list[0], (NB, N_COL * NNZ, BS, BS), (BS * NNZ * N_COL // 3) ** -0.5, 0.109375, ((0, 16), (1, 8)))
    columns = set_ends(jax.random.randint(key_list[1], (NB, N_COL * NNZ), 0, CB), jax.random.fold_in(key_list[1], 1), 0, CB - 1).astype(jnp.int32)
    counts = draw_counts(jax.random.fold_in(key_list[4], 71), 0)
    vectors = bell_draw(key_list[3], (NB, K, BS), 1.0, 6.0, ((0, 128),))
    return dict(blocks=blocks, columns=columns, counts=counts, vectors=vectors)


def slot_masks(columns, counts):
    slots = jnp.arange(N_COL * NNZ, dtype=jnp.int32)
    global_cols = columns.astype(jnp.int32) + ((slots // NNZ) * CB).astype(jnp.int32)[None, :]
    active = (slots % NNZ)[None, :] < jnp.repeat(counts, NNZ, axis=1)
    return global_cols.astype(jnp.int32), active.astype(jnp.float32)


def forward(blocks, global_cols, active, vectors):
    wide = vectors.astype(jnp.float32)

    def group_product(items):
        group_blocks, group_cols, group_active = items
        picked = wide[group_cols] * group_active[:, :, None, None]
        return jnp.einsum("isrc,iskc->ikr", group_blocks.astype(jnp.float32), picked)

    shaped = (blocks.reshape(N_ROW, RB, N_COL * NNZ, BS, BS),
              global_cols.reshape(N_ROW, RB, N_COL * NNZ),
              active.reshape(N_ROW, RB, N_COL * NNZ))
    result = lax.map(group_product, shaped)
    return result.reshape(NB, K, BS).astype(jnp.bfloat16)


def adjoint(blocks, global_cols, active, vectors):
    def group_step(summed, items):
        group_blocks, group_cols, group_active, group_vecs = items
        terms = jnp.einsum("isrc,ikr->iskc", group_blocks.astype(jnp.float32), group_vecs.astype(jnp.float32))
        terms = terms * group_active[:, :, None, None]
        added = jax.ops.segment_sum(terms.reshape(RB * N_COL * NNZ, K, BS), group_cols.reshape(RB * N_COL * NNZ), num_segments=NB)
        return summed + added, None

    shaped = (blocks.reshape(N_ROW, RB, N_COL * NNZ, BS, BS),
              global_cols.reshape(N_ROW, RB, N_COL * NNZ),
              active.reshape(N_ROW, RB, N_COL * NNZ),
              vectors.reshape(N_ROW, RB, K, BS))
    summed, unused = lax.scan(group_step, jnp.zeros((NB, K, BS), jnp.float32), shaped)
    return summed.astype(jnp.bfloat16)


def reference(blocks, columns, counts, vectors):
    global_cols, active = slot_masks(columns, counts)
    first_image = forward(blocks, global_cols, active, vectors)
    first_back = adjoint(blocks, global_cols, active, first_image)
    second_image = forward(blocks, global_cols, active, first_back)
    second_back = adjoint(blocks, global_cols, active, second_image)
    return (first_image, first_back, second_image, second_back)
```

```python
import functools

import jax
import jax.numpy as jnp
from jax import lax
from jax.experimental import pallas as pl
from jax.experimental.pallas import tpu as pltpu
from jax.sharding import PartitionSpec as P

MESH = pl.DeviceIdType.MESH
NT = (((1,), (1,)), ((), ()))
F32 = jnp.float32
BF16 = jnp.bfloat16


def kernel(
    n_row, n_col, vb,
    blocks, gcol, perm, keep, last, vectors,
    out0, out1, out2, out3,
    w, cv, pb, rb, rv, tb, seg, sb, sib, hb, rr,
    load_sem, ag_send, ag_recv, fw_send, fw_recv, sc_send, sc_recv,
    gc_send, gc_recv, sx_send, sx_recv, sr_send, sr_recv,
):
    row = lax.axis_index("row")
    col = lax.axis_index("col")
    chips = n_row // 2
    chip = row // 2
    core = row % 2
    nnz = w.shape[0] // (n_col * vb)
    rows = n_col * vb
    slots = rows * nnz
    cols = n_row * vb
    k, bs = vectors.shape[1], vectors.shape[2]

    def peer(step):
        return (chip + step) % chips

    def cpeer(step):
        return (col + step) % n_col

    def load(d):
        part = pl.ds(d * vb * nnz, vb * nnz)
        return pltpu.make_async_copy(blocks.at[part], w.at[part], load_sem.at[d])

    for d in range(n_col):
        load(d).start()

    barrier = pltpu.get_barrier_semaphore()
    pl.semaphore_signal(barrier, inc=1, device_id={"row": chip * 2 + 1 - core}, device_id_type=MESH)

    def greet_chip(s, c):
        pl.semaphore_signal(barrier, inc=1, device_id={"row": peer(s) * 2 + core}, device_id_type=MESH)
        return c

    def greet_col(s, c):
        pl.semaphore_signal(barrier, inc=1, device_id={"col": cpeer(s)}, device_id_type=MESH)
        return c

    lax.fori_loop(1, chips, greet_chip, 0)
    lax.fori_loop(1, n_col, greet_col, 0)
    pl.semaphore_wait(barrier, 1 + (chips - 1) + (n_col - 1))

    zero = jnp.zeros((k, bs), F32)
    seg[slots] = zero

    sibling = {"row": chip * 2 + 1 - core}

    for rnd in range(2):
        src = vectors if rnd == 0 else out1
        image = out0 if rnd == 0 else out2
        back = out1 if rnd == 0 else out3
        cvr = cv.at[rnd]
        rbr = rb.at[rnd]
        rvr = rv.at[rnd]
        sibr = sib.at[rnd]
        rrr = rr.at[rnd]
        cvr[cols] = zero.astype(BF16)

        def shard(r):
            return cvr.at[pl.ds(r * vb, vb)]

        def gather(s):
            return pltpu.make_async_remote_copy(
                src_ref=src, dst_ref=shard(row), send_sem=ag_send.at[rnd, s], recv_sem=ag_recv.at[rnd, s],
                device_id={"row": peer(s) * 2 + core}, device_id_type=MESH)

        def gather_arrival(s):
            there = (chip + chips - s) % chips
            return pltpu.make_async_remote_copy(
                src_ref=src, dst_ref=shard(there * 2 + core), send_sem=ag_send.at[rnd, s], recv_sem=ag_recv.at[rnd, s],
                device_id={"row": peer(s) * 2 + core}, device_id_type=MESH)

        def forwarding(s):
            there = (chip + chips - s) % chips
            at = shard(there * 2 + core)
            return pltpu.make_async_remote_copy(
                src_ref=at, dst_ref=at, send_sem=fw_send.at[rnd, s], recv_sem=fw_recv.at[rnd, s],
                device_id=sibling, device_id_type=MESH)

        def forwarding_arrival(s):
            there = (chip + chips - s) % chips
            at = shard(there * 2 + 1 - core)
            return pltpu.make_async_remote_copy(
                src_ref=at, dst_ref=at, send_sem=fw_send.at[rnd, s], recv_sem=fw_recv.at[rnd, s],
                device_id=sibling, device_id_type=MESH)

        def own_out():
            return pltpu.make_async_remote_copy(
                src_ref=src, dst_ref=shard(row), send_sem=fw_send.at[rnd, 0], recv_sem=fw_recv.at[rnd, 0],
                device_id=sibling, device_id_type=MESH)

        def gather_start(s, c):
            gather(s).start()
            return c

        own_out().start()
        lax.fori_loop(1, chips, gather_start, 0)
        shard(row)[...] = src[...]

        def pass_on(s, c):
            gather_arrival(s).wait_recv()
            forwarding(s).start()
            return c

        lax.fori_loop(1, chips, pass_on, 0)
        pltpu.make_async_remote_copy(
            src_ref=src, dst_ref=shard(chip * 2 + 1 - core), send_sem=fw_send.at[rnd, 0], recv_sem=fw_recv.at[rnd, 0],
            device_id=sibling, device_id_type=MESH).wait_recv()

        def gather_end(s, c):
            forwarding_arrival(s).wait_recv()
            forwarding(s).wait_send()
            gather(s).wait_send()
            return c

        own_out().wait_send()
        lax.fori_loop(1, chips, gather_end, 0)

        if rnd == 0:
            for d in range(n_col):
                load(d).wait()

        def partial(d):
            def one(i, c):
                base = (d * vb + i) * nnz
                x = jnp.concatenate([cvr[gcol[base + q]] for q in range(nnz)], axis=1)
                m = jnp.concatenate([w[base + q] for q in range(nnz)], axis=1)
                pb[rnd, d, i] = lax.dot_general(x, m, NT, preferred_element_type=F32).astype(BF16)
                return c
            lax.fori_loop(0, vb, one, 0, unroll=4)

        def scatter(s):
            return pltpu.make_async_remote_copy(
                src_ref=pb.at[rnd, cpeer(s)], dst_ref=rbr.at[s], send_sem=sc_send.at[rnd, s], recv_sem=sc_recv.at[rnd, s],
                device_id={"col": cpeer(s)}, device_id_type=MESH)

        def forward_step(s, c):
            partial(cpeer(s))
            scatter(s).start()
            return c

        lax.fori_loop(1, n_col, forward_step, 0)
        partial(col)

        def scatter_end(s, c):
            scatter(s).wait()
            return c

        lax.fori_loop(1, n_col, scatter_end, 0)

        def reduce_rows(i, c):
            total = pb[rnd, col, i].astype(F32)
            for s in range(1, n_col):
                total += rbr[s, i].astype(F32)
            total = total.astype(BF16)
            image[i] = total
            rvr[col * vb + i] = total
            return c

        lax.fori_loop(0, vb, reduce_rows, 0)

        def rshard(d):
            return rvr.at[pl.ds(d * vb, vb)]

        def spread(s):
            return pltpu.make_async_remote_copy(
                src_ref=rshard(col), dst_ref=rshard(col), send_sem=gc_send.at[rnd, s], recv_sem=gc_recv.at[rnd, s],
                device_id={"col": cpeer(s)}, device_id_type=MESH)

        def spread_arrival(s):
            at = rshard((col + n_col - s) % n_col)
            return pltpu.make_async_remote_copy(
                src_ref=at, dst_ref=at, send_sem=gc_send.at[rnd, s], recv_sem=gc_recv.at[rnd, s],
                device_id={"col": cpeer(s)}, device_id_type=MESH)

        def spread_start(s, c):
            spread(s).start()
            return c

        lax.fori_loop(1, n_col, spread_start, 0)

        def terms(d):
            def one(i, c):
                at = d * vb + i
                v = rvr[at]
                for q in range(0, nnz, 2):
                    base = at * nnz + q
                    m = jnp.concatenate([w[base], w[base + 1]], axis=1)
                    r = jnp.dot(v, m, preferred_element_type=F32)
                    tb[base] = r[:, :bs]
                    tb[base + 1] = r[:, bs:]
                return c
            lax.fori_loop(0, vb, one, 0, unroll=4)

        terms(col)

        def terms_step(s, c):
            spread_arrival(s).wait_recv()
            terms((col + n_col - s) % n_col)
            return c

        lax.fori_loop(1, n_col, terms_step, 0)

        def spread_end(s, c):
            spread(s).wait_send()
            return c

        lax.fori_loop(1, n_col, spread_end, 0)

        def running(t, total):
            total = total * keep[t] + tb[perm[t]]
            seg[t] = total
            return total

        lax.fori_loop(0, slots, running, zero, unroll=8)

        def column_chunk(r):
            def one(i, c):
                sb[rnd, r, i] = seg[last[r * vb + i]].astype(BF16)
                return c
            lax.fori_loop(0, vb, one, 0, unroll=4)

        def swap(q):
            return pltpu.make_async_remote_copy(
                src_ref=sb.at[rnd, q * 2 + 1 - core], dst_ref=sibr.at[q], send_sem=sx_send.at[rnd, q], recv_sem=sx_recv.at[rnd, q],
                device_id=sibling, device_id_type=MESH)

        def swap_step(s, c):
            q = peer(s)
            column_chunk(q * 2 + 1 - core)
            swap(q).start()
            return c

        lax.fori_loop(1, chips + 1, swap_step, 0)

        def own_step(s, c):
            column_chunk(peer(s) * 2 + core)
            return c

        lax.fori_loop(1, chips + 1, own_step, 0)

        def scatter_row(s):
            return pltpu.make_async_remote_copy(
                src_ref=hb.at[rnd, s], dst_ref=rrr.at[s], send_sem=sr_send.at[rnd, s], recv_sem=sr_recv.at[rnd, s],
                device_id={"row": peer(s) * 2 + core}, device_id_type=MESH)

        def pair_step(s, c):
            q = peer(s)
            swap(q).wait()
            hb[rnd, s] = (sb[rnd, q * 2 + core].astype(F32) + sibr[q].astype(F32)).astype(BF16)
            scatter_row(s).start()
            return c

        lax.fori_loop(1, chips, pair_step, 0)
        swap(chip).wait()

        def scatter_row_end(s, c):
            scatter_row(s).wait()
            return c

        lax.fori_loop(1, chips, scatter_row_end, 0)

        def reduce_cols(i, c):
            total = sb[rnd, row, i].astype(F32) + sibr[chip, i].astype(F32)
            for s in range(1, chips):
                total += rrr[s, i].astype(F32)
            back[i] = total.astype(BF16)
            return c

        lax.fori_loop(0, vb, reduce_cols, 0)


def column_order(col, col_count):
    slots = col.shape[0]
    ids = jnp.arange(slots, dtype=jnp.int32)
    key = col * slots + ids
    rank = jnp.sum((key[None, :] < key[:, None]).astype(jnp.int32), axis=1)
    hit = (rank[:, None] == ids[None, :]).astype(jnp.int32)
    perm = jnp.sum(hit * ids[:, None], axis=0)
    ordered = jnp.sum(hit * col[:, None], axis=0)
    before = jnp.concatenate([jnp.full((1,), -1, jnp.int32), ordered[:-1]])
    keep = (ordered == before).astype(F32)
    js = jnp.arange(col_count, dtype=jnp.int32)
    upto = jnp.sum((col[None, :] <= js[:, None]).astype(jnp.int32), axis=1)
    some = jnp.sum((col[None, :] == js[:, None]).astype(jnp.int32), axis=1)
    last = jnp.where(some > 0, upto - 1, slots)
    return perm, keep, last


def body(n_row, n_col, blocks, columns, counts, vectors):
    rows, nnz, bs, _ = blocks.shape
    vb, k, _ = vectors.shape
    slots = rows * nnz
    cols = n_row * vb
    chips = n_row // 2
    active = jnp.arange(nnz, dtype=jnp.int32)[None, :] < counts
    gcol = jnp.where(active, columns, cols).astype(jnp.int32).reshape(slots)
    perm, keep, last = column_order(gcol, cols)
    any_space = pl.BlockSpec(memory_space=pl.ANY)
    smem = pl.BlockSpec(memory_space=pltpu.SMEM)
    vmem = pl.BlockSpec(memory_space=pltpu.VMEM)
    dma = pltpu.SemaphoreType.DMA
    outs = pl.pallas_call(
        functools.partial(kernel, n_row, n_col, vb),
        out_shape=[jax.ShapeDtypeStruct((vb, k, bs), BF16)] * 4,
        in_specs=[any_space, smem, smem, smem, smem, vmem],
        out_specs=[vmem] * 4,
        scratch_shapes=[
            pltpu.VMEM((slots, bs, bs), BF16),
            pltpu.VMEM((2, cols + 1, k, bs), BF16),
            pltpu.VMEM((2, n_col, vb, k, bs), BF16),
            pltpu.VMEM((2, n_col, vb, k, bs), BF16),
            pltpu.VMEM((2, rows, k, bs), BF16),
            pltpu.VMEM((slots, k, bs), F32),
            pltpu.VMEM((slots + 1, k, bs), F32),
            pltpu.VMEM((2, n_row, vb, k, bs), BF16),
            pltpu.VMEM((2, chips, vb, k, bs), BF16),
            pltpu.VMEM((2, chips, vb, k, bs), BF16),
            pltpu.VMEM((2, chips, vb, k, bs), BF16),
            dma((n_col,)),
            dma((2, chips)), dma((2, chips)),
            dma((2, chips)), dma((2, chips)),
            dma((2, n_col)), dma((2, n_col)),
            dma((2, n_col)), dma((2, n_col)),
            dma((2, chips)), dma((2, chips)),
            dma((2, chips)), dma((2, chips)),
        ],
        compiler_params=pltpu.CompilerParams(
            collective_id=0, has_side_effects=True, vmem_limit_bytes=56 << 20),
        name="krylov",
    )(blocks.reshape(slots, bs, bs), gcol, perm, keep, last, vectors)
    return tuple(outs)


def solution(mesh):
    in_specs = (
        P("row", "col", None, None),
        P("row", "col"),
        P("row", "col"),
        P(("col", "row"), None, None),
    )
    out_specs = (
        P(("row", "col"), None, None),
        P(("col", "row"), None, None),
        P(("row", "col"), None, None),
        P(("col", "row"), None, None),
    )
    run = functools.partial(body, mesh.shape["row"], mesh.shape["col"])
    return jax.shard_map(run, mesh=mesh, in_specs=in_specs, out_specs=out_specs, check_vma=False)
```

```python
import functools

import jax
import jax.numpy as jnp
from jax import lax
from jax.experimental import pallas as pl
from jax.experimental.pallas import tpu as pltpu
from jax.sharding import PartitionSpec as P

MESH = pl.DeviceIdType.MESH
F32 = jnp.float32
BF16 = jnp.bfloat16


def kernel(
    n_row, n_col, vb,
    blocks, gcol, perm, keep, last, vectors,
    out0, out1, out2, out3,
    w, wt, cv0, cv1, cv2, cv3, pb, rb, rv, tb, seg, sb, sib, hb, rr,
    load_sem, ag_send, ag_recv, fw_send, fw_recv, sc_send, sc_recv,
    gc_send, gc_recv, sx_send, sx_recv, sr_send, sr_recv,
):
    row = lax.axis_index("row")
    col = lax.axis_index("col")
    chips = n_row // 2
    nx, nz = chips // 2, n_col // 2
    chip, core = row // 2, row % 2
    x, y = chip // 2, chip % 2
    h, z = col // nz, col % nz
    rows = n_col * vb
    nnz = w.shape[0] // rows
    slots = rows * nnz
    cols = n_row * vb
    k2, bs = vectors.shape[1] // 2, vectors.shape[2]
    sibling = {"row": chip * 2 + 1 - core}

    def chip_to(e):
        return ((x + e % nx) % nx) * 2 + (y + e // nx) % 2

    def chip_from(e):
        return ((x + nx - e % nx) % nx) * 2 + (y + e // nx) % 2

    def col_to(e):
        return ((h + e // nz) % 2) * nz + (z + e % nz) % nz

    def col_from(e):
        return ((h + e // nz) % 2) * nz + (z + nz - e % nz) % nz

    def far_first(n, step):
        def one(s, c):
            step(n - 1 - s)
            return c
        lax.fori_loop(0, n - 1, one, 0)

    def load(d):
        part = pl.ds(d * vb * nnz, vb * nnz)
        return pltpu.make_async_copy(blocks.at[part], w.at[part], load_sem.at[d])

    for d in range(n_col):
        load(d).start()

    barrier = pltpu.get_barrier_semaphore()
    pl.semaphore_signal(barrier, inc=1, device_id=sibling, device_id_type=MESH)

    def greet_chip(e):
        pl.semaphore_signal(barrier, inc=1, device_id={"row": chip_to(e) * 2 + core}, device_id_type=MESH)

    def greet_col(e):
        pl.semaphore_signal(barrier, inc=1, device_id={"col": col_to(e)}, device_id_type=MESH)

    far_first(chips, greet_chip)
    far_first(n_col, greet_col)

    zero = jnp.zeros((k2, bs), F32)
    seg[slots] = zero

    class Part:
        def __init__(self, rnd, half):
            self.at = rnd * 2 + half
            self.mine = pl.ds(half * k2, k2)
            self.image = out0 if rnd == 0 else out2
            self.back = out1 if rnd == 0 else out3
            self.cv = (cv0, cv1, cv2, cv3)[self.at]
            self.pb, self.rb, self.rv = pb.at[self.at], rb.at[self.at], rv.at[self.at]
            self.sb, self.sib = sb.at[self.at], sib.at[self.at]
            self.hb, self.rr = hb.at[self.at], rr.at[self.at]

        def shard(self, r):
            return self.cv.at[pl.ds(r * vb, vb)]

        def copy(self, src, dst, send, recv, j, to):
            return pltpu.make_async_remote_copy(
                src_ref=src, dst_ref=dst, send_sem=send.at[self.at, j], recv_sem=recv.at[self.at, j],
                device_id=to, device_id_type=MESH)

        def gather(self, e, owner=None):
            at = self.shard(row if owner is None else owner)
            return self.copy(at, at, ag_send, ag_recv, e, {"row": chip_to(e) * 2 + core})

        def forwarding(self, e, owner):
            at = self.shard(owner)
            return self.copy(at, at, fw_send, fw_recv, e, sibling)

        def gather_start(self):
            self.cv[cols] = zero.astype(BF16)
            far_first(chips, lambda e: self.gather(e).start())
            self.forwarding(0, row).start()

        def pass_on(self):
            def one(s, c):
                e = s + 1
                owner = chip_from(e) * 2 + core
                self.gather(e, owner).wait_recv()
                self.forwarding(e, owner).start()
                return c
            lax.fori_loop(0, chips - 1, one, 0)

        def gather_end(self):
            def one(e, c):
                self.forwarding(e, chip_from(e) * 2 + 1 - core).wait_recv()
                return c
            lax.fori_loop(0, chips, one, 0)

        def partial(self, d):
            for i in range(vb):
                base = (d * vb + i) * nnz
                v = jnp.concatenate([self.cv[gcol[base + q]] for q in range(nnz)], axis=1)
                m = wt[pl.ds(base, nnz)].reshape(nnz * bs, bs)
                self.pb[d, i] = jnp.dot(v, m, preferred_element_type=F32).astype(BF16)

        def scatter(self, e):
            return self.copy(self.pb.at[col_to(e)], self.rb.at[e], sc_send, sc_recv, e, {"col": col_to(e)})

        def forward(self):
            def one(s, c):
                e = n_col - 1 - s
                self.partial(col_to(e))

                @pl.when(e > 0)
                def _():
                    self.scatter(e).start()
                return c
            lax.fori_loop(0, n_col, one, 0)

        def reduce_rows(self):
            far_first(n_col, lambda e: self.scatter(e).wait_recv())
            for i in range(vb):
                total = self.pb[col, i].astype(F32)
                for e in range(1, n_col):
                    total += self.rb[e, i].astype(F32)
                total = total.astype(BF16)
                self.image[i, self.mine] = total
                self.rv[col * vb + i] = total
            far_first(n_col, lambda e: self.spread(e).start())

        def spread(self, e, owner=None):
            at = self.rv.at[pl.ds((col if owner is None else owner) * vb, vb)]
            return self.copy(at, at, gc_send, gc_recv, e, {"col": col_to(e)})

        def terms(self, first, end):
            def one(e, c):
                d = col_from(e)

                @pl.when(e > 0)
                def _():
                    self.spread(e, d).wait_recv()
                for i in range(vb):
                    at = d * vb + i
                    v = self.rv[at]
                    for q in range(0, nnz, 2):
                        base = at * nnz + q
                        m = jnp.concatenate([w[base], w[base + 1]], axis=1)
                        r = jnp.dot(v, m, preferred_element_type=F32)
                        tb[base] = r[:, :bs]
                        tb[base + 1] = r[:, bs:]
                return c
            lax.fori_loop(first, end, one, 0)

        def column_chunk(self, r):
            for i in range(vb):
                self.sb[r, i] = seg[last[r * vb + i]].astype(BF16)

        def swap(self, q):
            return self.copy(self.sb.at[q * 2 + 1 - core], self.sib.at[q], sx_send, sx_recv, q, sibling)

        def combine(self):
            def running(t, total):
                total = total * keep[t] + tb[perm[t]]
                seg[t] = total
                return total

            lax.fori_loop(0, slots, running, zero, unroll=16)

            def theirs(s, c):
                q = chip_to(chips - 1 - s)
                self.column_chunk(q * 2 + 1 - core)
                self.swap(q).start()
                return c

            def ours(r, c):
                self.column_chunk(r * 2 + core)
                return c

            lax.fori_loop(0, chips, theirs, 0)
            lax.fori_loop(0, chips, ours, 0)

        def scatter_row(self, e):
            return self.copy(self.hb.at[e], self.rr.at[e], sr_send, sr_recv, e, {"row": chip_to(e) * 2 + core})

        def pair(self):
            def one(e):
                q = chip_to(e)
                self.swap(q).wait_recv()
                self.hb[e] = (self.sb[q * 2 + core].astype(F32) + self.sib[q].astype(F32)).astype(BF16)
                self.scatter_row(e).start()
            far_first(chips, one)
            self.swap(chip).wait_recv()

        def reduce_cols(self, following):
            far_first(chips, lambda e: self.scatter_row(e).wait_recv())
            for i in range(vb):
                total = self.sb[row, i].astype(F32) + self.sib[chip, i].astype(F32)
                for e in range(1, chips):
                    total += self.rr[e, i].astype(F32)
                total = total.astype(BF16)
                self.back[i, self.mine] = total
                if following is not None:
                    following.cv[row * vb + i] = total
            if following is not None:
                following.gather_start()

        def end(self):
            def by_chip(e):
                self.gather(e).wait_send()
                self.forwarding(e, row).wait_send()
                self.scatter_row(e).wait_send()
                self.swap(e).wait_send()

            def by_col(e):
                self.scatter(e).wait_send()
                self.spread(e).wait_send()

            far_first(chips, by_chip)
            far_first(n_col, by_col)
            self.forwarding(0, row).wait_send()
            self.swap(0).wait_send()

    parts = [[Part(rnd, half) for half in range(2)] for rnd in range(2)]
    a, b = parts[0]
    for part in (a, b):
        for i in range(vb):
            part.cv[row * vb + i] = vectors[i, part.mine]
    pl.semaphore_wait(barrier, 1 + (chips - 1) + (n_col - 1))
    a.gather_start()
    b.gather_start()

    def turn(d, c):
        load(d).wait()

        def one(i, cc):
            wt[d * vb * nnz + i] = w[d * vb * nnz + i].T
            return cc
        lax.fori_loop(0, vb * nnz, one, 0, unroll=8)
        return c

    early = n_col - n_col // 4
    lax.fori_loop(0, early, turn, 0)
    a.pass_on()
    lax.fori_loop(early, n_col, turn, 0)

    for rnd in range(2):
        a, b = parts[rnd]
        a.gather_end()
        a.forward()
        b.pass_on()
        b.gather_end()
        b.forward()
        a.reduce_rows()
        b.reduce_rows()
        a.terms(0, n_col)
        a.combine()
        b.terms(0, n_col // 2)
        a.pair()
        b.terms(n_col // 2, n_col)
        b.combine()
        b.pair()
        following = parts[1] if rnd == 0 else (None, None)
        a.reduce_cols(following[0])
        b.reduce_cols(following[1])
        if rnd == 0:
            following[0].pass_on()

    for pair in parts:
        for part in pair:
            part.end()


def copy_out(*refs):
    n = len(refs) // 2
    for j in range(n):
        refs[n + j][...] = refs[j][...]


def column_order(col, col_count):
    slots = col.shape[0]
    ids = jnp.arange(slots, dtype=jnp.int32)
    key = col * slots + ids
    rank = jnp.sum((key[None, :] < key[:, None]).astype(jnp.int32), axis=1)
    hit = (rank[:, None] == ids[None, :]).astype(jnp.int32)
    perm = jnp.sum(hit * ids[:, None], axis=0)
    ordered = jnp.sum(hit * col[:, None], axis=0)
    before = jnp.concatenate([jnp.full((1,), -1, jnp.int32), ordered[:-1]])
    keep = (ordered == before).astype(F32)
    js = jnp.arange(col_count, dtype=jnp.int32)
    upto = jnp.sum((col[None, :] <= js[:, None]).astype(jnp.int32), axis=1)
    some = jnp.sum((col[None, :] == js[:, None]).astype(jnp.int32), axis=1)
    last = jnp.where(some > 0, upto - 1, slots)
    return perm, keep, last


def body(n_row, n_col, blocks, columns, counts, vectors):
    rows, nnz, bs, _ = blocks.shape
    vb, k, _ = vectors.shape
    k2 = k // 2
    slots = rows * nnz
    cols = n_row * vb
    chips = n_row // 2
    active = jnp.arange(nnz, dtype=jnp.int32)[None, :] < counts
    gcol = jnp.where(active, columns, cols).astype(jnp.int32).reshape(slots)
    perm, keep, last = column_order(gcol, cols)
    any_space = pl.BlockSpec(memory_space=pl.ANY)
    smem = pl.BlockSpec(memory_space=pltpu.SMEM)
    vmem = pl.BlockSpec(memory_space=pltpu.VMEM)
    dma = pltpu.SemaphoreType.DMA
    result = [jax.ShapeDtypeStruct((vb, k, bs), BF16)] * 4
    outs = pl.pallas_call(
        functools.partial(kernel, n_row, n_col, vb),
        out_shape=result,
        in_specs=[any_space, smem, smem, smem, smem, vmem],
        out_specs=[vmem] * 4,
        scratch_shapes=[
            pltpu.VMEM((slots, bs, bs), BF16),
            pltpu.VMEM((slots, bs, bs), BF16),
            *[pltpu.VMEM((cols + 1, k2, bs), BF16)] * 4,
            pltpu.VMEM((4, n_col, vb, k2, bs), BF16),
            pltpu.VMEM((4, n_col, vb, k2, bs), BF16),
            pltpu.VMEM((4, rows, k2, bs), BF16),
            pltpu.VMEM((slots, k2, bs), F32),
            pltpu.VMEM((slots + 1, k2, bs), F32),
            pltpu.VMEM((4, n_row, vb, k2, bs), BF16),
            pltpu.VMEM((4, chips, vb, k2, bs), BF16),
            pltpu.VMEM((4, chips, vb, k2, bs), BF16),
            pltpu.VMEM((4, chips, vb, k2, bs), BF16),
            dma((n_col,)),
            dma((4, chips)), dma((4, chips)),
            dma((4, chips)), dma((4, chips)),
            dma((4, n_col)), dma((4, n_col)),
            dma((4, n_col)), dma((4, n_col)),
            dma((4, chips)), dma((4, chips)),
            dma((4, chips)), dma((4, chips)),
        ],
        compiler_params=pltpu.CompilerParams(
            collective_id=0, has_side_effects=True, vmem_limit_bytes=58 << 20),
        name="krylov",
    )(blocks.reshape(slots, bs, bs), gcol, perm, keep, last, vectors)
    outs = pl.pallas_call(
        copy_out,
        out_shape=result,
        in_specs=[vmem] * 4,
        out_specs=[vmem] * 4,
        name="results",
    )(*outs)
    return tuple(outs)


def solution(mesh):
    in_specs = (
        P("row", "col", None, None),
        P("row", "col"),
        P("row", "col"),
        P(("col", "row"), None, None),
    )
    out_specs = (
        P(("row", "col"), None, None),
        P(("col", "row"), None, None),
        P(("row", "col"), None, None),
        P(("col", "row"), None, None),
    )
    run = functools.partial(body, mesh.shape["row"], mesh.shape["col"])
    return jax.shard_map(run, mesh=mesh, in_specs=in_specs, out_specs=out_specs, check_vma=False)
```

```python
import functools

import jax
import jax.numpy as jnp
from jax import lax
from jax.experimental import pallas as pl
from jax.experimental.pallas import tpu as pltpu
from jax.sharding import PartitionSpec as P

MESH = pl.DeviceIdType.MESH
F32 = jnp.float32
BF16 = jnp.bfloat16


def kernel(
    n_row, n_col, vb,
    blocks, columns, vectors,
    out0, out1, out2, out3,
    perm_v, keep_v, last_v, perm, keep, last, gcol,
    w, wt, cv0, cv1, cv2, cv3, pb, rb, rv, tb0, tb1, seg, sb, sib, hb, rr,
    load_sem, order_sem, ag_send, ag_recv, fw_send, fw_recv, sc_send, sc_recv,
    gc_send, gc_recv, sx_send, sx_recv, sr_send, sr_recv,
):
    row = lax.axis_index("row")
    col = lax.axis_index("col")
    chips = n_row // 2
    nx, nz = chips // 2, n_col // 2
    chip, core = row // 2, row % 2
    x, y = chip // 2, chip % 2
    h, z = col // nz, col % nz
    rows = n_col * vb
    nnz = w.shape[0] // rows
    slots = rows * nnz
    cols = n_row * vb
    k2, bs = vectors.shape[1] // 2, vectors.shape[2]
    sibling = {"row": chip * 2 + 1 - core}

    def chip_to(e):
        return ((x + e % nx) % nx) * 2 + (y + e // nx) % 2

    def chip_from(e):
        return ((x + nx - e % nx) % nx) * 2 + (y + e // nx) % 2

    def col_to(e):
        return ((h + e // nz) % 2) * nz + (z + e % nz) % nz

    def col_from(e):
        return ((h + e // nz) % 2) * nz + (z + nz - e % nz) % nz

    def hops(e, ring, across):
        return min(e % ring, ring - e % ring) + across * (e // ring)

    far_chips = sorted(range(1, chips), key=lambda e: -hops(e, nx, 1))
    far_cols = sorted(range(1, n_col), key=lambda e: -hops(e, nz, 2))

    def each_chip(step):
        for e in far_chips:
            step(e)

    def each_col(step):
        for e in far_cols:
            step(e)

    def load(d):
        part = pl.ds(d * vb * nnz, vb * nnz)
        return pltpu.make_async_copy(blocks.at[part], w.at[part], load_sem.at[d])

    for d in range(n_col):
        load(d).start()

    barrier = pltpu.get_barrier_semaphore()
    pl.semaphore_signal(barrier, inc=1, device_id=sibling, device_id_type=MESH)

    def greet_chip(e):
        pl.semaphore_signal(barrier, inc=1, device_id={"row": chip_to(e) * 2 + core}, device_id_type=MESH)

    def greet_col(e):
        pl.semaphore_signal(barrier, inc=1, device_id={"col": col_to(e)}, device_id_type=MESH)

    each_chip(greet_chip)
    each_col(greet_col)

    zero = jnp.zeros((k2, bs), F32)
    seg[slots] = zero.astype(BF16)

    class Part:
        def __init__(self, rnd, half):
            self.at = rnd * 2 + half
            self.mine = pl.ds(half * k2, k2)
            self.image = out0 if rnd == 0 else out2
            self.back = out1 if rnd == 0 else out3
            self.cv = (cv0, cv1, cv2, cv3)[self.at]
            self.tb = (tb0, tb1)[half]
            self.pb, self.rb, self.rv = pb.at[self.at], rb.at[self.at], rv.at[self.at]
            self.sb, self.sib = sb.at[self.at], sib.at[self.at]
            self.hb, self.rr = hb.at[self.at], rr.at[self.at]

        def shard(self, r):
            return self.cv.at[pl.ds(r * vb, vb)]

        def copy(self, src, dst, send, recv, j, to):
            return pltpu.make_async_remote_copy(
                src_ref=src, dst_ref=dst, send_sem=send.at[self.at, j], recv_sem=recv.at[self.at, j],
                device_id=to, device_id_type=MESH)

        def gather(self, e, owner=None):
            at = self.shard(row if owner is None else owner)
            return self.copy(at, at, ag_send, ag_recv, e, {"row": chip_to(e) * 2 + core})

        def forwarding(self, e, owner):
            at = self.shard(owner)
            return self.copy(at, at, fw_send, fw_recv, e, sibling)

        def gather_start(self):
            self.cv[cols] = zero.astype(BF16)
            each_chip(lambda e: self.gather(e).start())
            self.forwarding(0, row).start()

        def pass_on(self, first, end):
            def one(e, c):
                owner = chip_from(e) * 2 + core
                self.gather(e, owner).wait_recv()
                self.forwarding(e, owner).start()
                return c
            lax.fori_loop(first, end, one, 0)

        def gather_end(self):
            def one(e, c):
                self.forwarding(e, chip_from(e) * 2 + 1 - core).wait_recv()
                return c
            lax.fori_loop(0, chips, one, 0)

        def partial(self, d):
            done = []
            for i in range(vb):
                base = (d * vb + i) * nnz
                v = jnp.concatenate([self.cv[gcol[0, base + q]] for q in range(nnz)], axis=1)
                m = wt[pl.ds(base, nnz)].reshape(nnz * bs, bs)
                done.append(jnp.dot(v, m, preferred_element_type=F32).astype(BF16))
            for i in range(vb):
                self.pb[d, i] = done[i]

        def scatter(self, e):
            return self.copy(self.pb.at[col_to(e)], self.rb.at[e], sc_send, sc_recv, e, {"col": col_to(e)})

        def forward(self, first, end):
            def one(s, c):
                e = n_col - 1 - s
                self.partial(col_to(e))

                @pl.when(e > 0)
                def _():
                    self.scatter(e).start()
                return c
            lax.fori_loop(first, end, one, 0)

        def reduce_rows(self):
            each_col(lambda e: self.scatter(e).wait_recv())
            total = self.pb[col].astype(F32)
            for e in range(1, n_col):
                total += self.rb[e].astype(F32)
            total = total.astype(BF16)
            self.rv[pl.ds(col * vb, vb)] = total
            each_col(lambda e: self.spread(e).start())
            self.image[:, self.mine] = total

        def spread(self, e, owner=None):
            at = self.rv.at[pl.ds((col if owner is None else owner) * vb, vb)]
            return self.copy(at, at, gc_send, gc_recv, e, {"col": col_to(e)})

        def terms(self, first, end):
            def one(e, c):
                d = col_from(e)

                @pl.when(e > 0)
                def _():
                    self.spread(e, d).wait_recv()
                for i in range(vb):
                    at = d * vb + i
                    v = self.rv[at]
                    done = []
                    for q in range(0, nnz, 2):
                        base = at * nnz + q
                        m = jnp.concatenate([w[base], w[base + 1]], axis=1)
                        r = jnp.dot(v, m, preferred_element_type=F32)
                        done += [r[:, :bs], r[:, bs:]]
                    for q in range(nnz):
                        self.tb[at * nnz + q] = done[q]
                return c
            lax.fori_loop(first, end, one, 0)

        def column_chunk(self, r):
            ends = [seg[last[0, r * vb + i]] for i in range(vb)]
            for i in range(vb):
                self.sb[r, i] = ends[i]

        def swap(self, q):
            return self.copy(self.sb.at[q * 2 + 1 - core], self.sib.at[q], sx_send, sx_recv, q, sibling)

        def combine(self):
            def running(u, total):
                read = [self.tb[perm[0, u * 16 + q]] for q in range(16)]
                sums = []
                for first in range(0, 16, 4):
                    chain, value = None, None
                    for q in range(first, first + 4):
                        stay = keep[0, u * 16 + q]
                        chain = stay if q == first else chain * stay
                        value = read[q] if q == first else value * stay + read[q]
                        sums.append(total * chain + value)
                    total = sums[-1]
                for q in range(16):
                    seg[u * 16 + q] = sums[q].astype(BF16)
                return total

            lax.fori_loop(0, slots // 16, running, zero)

            def theirs(s, c):
                q = chip_to(chips - 1 - s)
                self.column_chunk(q * 2 + 1 - core)
                self.swap(q).start()
                return c

            def ours(r, c):
                self.column_chunk(r * 2 + core)
                return c

            lax.fori_loop(0, chips, theirs, 0)
            lax.fori_loop(0, chips, ours, 0)

        def scatter_row(self, e):
            return self.copy(self.hb.at[e], self.rr.at[e], sr_send, sr_recv, e, {"row": chip_to(e) * 2 + core})

        def pair(self):
            def one(e):
                q = chip_to(e)
                self.swap(q).wait_recv()
                self.hb[e] = (self.sb[q * 2 + core].astype(F32) + self.sib[q].astype(F32)).astype(BF16)
                self.scatter_row(e).start()
            each_chip(one)
            self.swap(chip).wait_recv()

        def reduce_cols(self, following):
            each_chip(lambda e: self.scatter_row(e).wait_recv())
            total = self.sb[row].astype(F32) + self.sib[chip].astype(F32)
            for e in range(1, chips):
                total += self.rr[e].astype(F32)
            total = total.astype(BF16)
            if following is not None:
                following.cv[pl.ds(row * vb, vb)] = total
                following.gather_start()
            self.back[:, self.mine] = total

        def end(self):
            def by_chip(e):
                self.gather(e).wait_send()
                self.forwarding(e, row).wait_send()
                self.scatter_row(e).wait_send()
                self.swap(e).wait_send()

            def by_col(e):
                self.scatter(e).wait_send()
                self.spread(e).wait_send()

            each_chip(by_chip)
            each_col(by_col)
            self.forwarding(0, row).wait_send()
            self.swap(0).wait_send()

    parts = [[Part(rnd, half) for half in range(2)] for rnd in range(2)]
    a, b = parts[0]
    for part in (a, b):
        for i in range(vb):
            part.cv[row * vb + i] = vectors[i, part.mine]
    pl.semaphore_wait(barrier, 1 + (chips - 1) + (n_col - 1))
    a.gather_start()
    b.gather_start()

    def turn(d, c):
        load(d).wait()

        def one(i, cc):
            wt[d * vb * nnz + i] = w[d * vb * nnz + i].T
            return cc
        lax.fori_loop(0, vb * nnz, one, 0, unroll=8)
        return c

    column_order(columns, nnz, cols, perm_v, keep_v, last_v)
    moves = [
        pltpu.make_async_copy(src, dst, order_sem.at[j])
        for j, (src, dst) in enumerate(((perm_v, perm), (keep_v, keep), (last_v, last), (columns, gcol)))
    ]
    for move in moves:
        move.start()
    for move in moves:
        move.wait()

    early = n_col - n_col // 4
    lax.fori_loop(0, early, turn, 0)
    a.pass_on(1, chips)
    lax.fori_loop(early, n_col, turn, 0)

    near, half = (chips + 1) // 2, n_col // 2
    for rnd in range(2):
        a, b = parts[rnd]
        a.gather_end()
        cut = n_col - n_col // 4 if rnd == 0 else n_col
        a.forward(0, cut)
        b.pass_on(1, chips)
        a.forward(cut, n_col)
        b.gather_end()
        b.forward(0, n_col)
        a.reduce_rows()
        a.terms(0, 1)
        if rnd == 1:
            for part in parts[0]:
                part.end()
        b.reduce_rows()
        b.terms(0, 1)
        a.terms(1, n_col)
        a.combine()
        b.terms(1, half)
        a.pair()
        b.terms(half, n_col)
        b.combine()
        b.pair()
        if rnd == 0:
            a.reduce_cols(parts[1][0])
            parts[1][0].pass_on(1, near)
            b.reduce_cols(parts[1][1])
            parts[1][0].pass_on(near, chips)
        else:
            a.end()
            a.reduce_cols(None)
            b.end()
            b.reduce_cols(None)


def copy_out(*refs):
    n = len(refs) // 2
    for j in range(n):
        refs[n + j][...] = refs[j][...]


def column_order(columns, nnz, col_count, perm, keep, last):
    slots = columns.shape[1]
    rows = slots // nnz
    ts = lax.broadcasted_iota(jnp.int32, (rows, slots), 1)
    block_row = lax.broadcasted_iota(jnp.int32, (rows, slots), 0)
    parts = [
        jnp.sum(jnp.where(block_row * nnz + q == ts, columns[...], 0), axis=1, keepdims=True)
        for q in range(nnz)
    ]
    js = lax.broadcasted_iota(jnp.int32, (rows, col_count), 1)
    ones = jnp.concatenate([(part == js).astype(jnp.int32) for part in parts], axis=0)
    below = sum(jnp.sum((part < js).astype(jnp.int32), axis=0, keepdims=True) for part in parts)
    upto = ones
    step = 1
    while step < slots:
        upto = upto + jnp.concatenate([jnp.zeros((step, col_count), jnp.int32), upto[:slots - step]], axis=0)
        step *= 2
    held = upto[slots - 1:]
    last[...] = jnp.where(held > 0, below + held - 1, slots)
    found, follows = 0, 0
    for q, part in enumerate(parts):
        at = slice(q * rows, (q + 1) * rows)
        before = jnp.sum(ones[at] * (upto[at] - 1), axis=1, keepdims=True)
        rank = before + jnp.sum(ones[at] * below, axis=1, keepdims=True)
        rank = jnp.where(part < col_count, rank, slots)
        slot = block_row * nnz + q
        hit = rank == ts
        found += jnp.sum(jnp.where(hit, slot, 0), axis=0, keepdims=True)
        follows += jnp.sum(jnp.where(hit & (before > 0), 1, 0), axis=0, keepdims=True)
    perm[...] = found
    keep[...] = follows.astype(F32)


def body(n_row, n_col, blocks, columns, counts, vectors):
    rows, nnz, bs, _ = blocks.shape
    vb, k, _ = vectors.shape
    k2 = k // 2
    slots = rows * nnz
    cols = n_row * vb
    chips = n_row // 2
    active = jnp.arange(nnz, dtype=jnp.int32)[None, :] < counts
    gcol = jnp.where(active, columns, cols).astype(jnp.int32).reshape(1, slots)
    any_space = pl.BlockSpec(memory_space=pl.ANY)
    vmem = pl.BlockSpec(memory_space=pltpu.VMEM)
    dma = pltpu.SemaphoreType.DMA
    order = [((1, slots), jnp.int32), ((1, slots), F32), ((1, cols), jnp.int32)]
    result = [jax.ShapeDtypeStruct((vb, k, bs), BF16)] * 4
    outs = pl.pallas_call(
        functools.partial(kernel, n_row, n_col, vb),
        out_shape=result,
        in_specs=[any_space, vmem, vmem],
        out_specs=[vmem] * 4,
        scratch_shapes=[
            *[space(shape, kind) for space in (pltpu.VMEM, pltpu.SMEM) for shape, kind in order],
            pltpu.SMEM((1, slots), jnp.int32),
            pltpu.VMEM((slots, bs, bs), BF16),
            pltpu.VMEM((slots, bs, bs), BF16),
            *[pltpu.VMEM((cols + 1, k2, bs), BF16)] * 4,
            pltpu.VMEM((4, n_col, vb, k2, bs), BF16),
            pltpu.VMEM((4, n_col, vb, k2, bs), BF16),
            pltpu.VMEM((4, rows, k2, bs), BF16),
            *[pltpu.VMEM((slots, k2, bs), F32)] * 2,
            pltpu.VMEM((slots + 1, k2, bs), BF16),
            pltpu.VMEM((4, n_row, vb, k2, bs), BF16),
            pltpu.VMEM((4, chips, vb, k2, bs), BF16),
            pltpu.VMEM((4, chips, vb, k2, bs), BF16),
            pltpu.VMEM((4, chips, vb, k2, bs), BF16),
            dma((n_col,)), dma((4,)),
            dma((4, chips)), dma((4, chips)),
            dma((4, chips)), dma((4, chips)),
            dma((4, n_col)), dma((4, n_col)),
            dma((4, n_col)), dma((4, n_col)),
            dma((4, chips)), dma((4, chips)),
            dma((4, chips)), dma((4, chips)),
        ],
        compiler_params=pltpu.CompilerParams(
            collective_id=0, has_side_effects=True, vmem_limit_bytes=58 << 20),
        name="krylov",
    )(blocks.reshape(slots, bs, bs), gcol, vectors)
    outs = pl.pallas_call(
        copy_out,
        out_shape=result,
        in_specs=[vmem] * 4,
        out_specs=[vmem] * 4,
        name="results",
    )(*outs)
    return tuple(outs)


def solution(mesh):
    in_specs = (
        P("row", "col", None, None),
        P("row", "col"),
        P("row", "col"),
        P(("col", "row"), None, None),
    )
    out_specs = (
        P(("row", "col"), None, None),
        P(("col", "row"), None, None),
        P(("row", "col"), None, None),
        P(("col", "row"), None, None),
    )
    run = functools.partial(body, mesh.shape["row"], mesh.shape["col"])
    return jax.shard_map(run, mesh=mesh, in_specs=in_specs, out_specs=out_specs, check_vma=False)
```

```python
import functools

import jax
import jax.numpy as jnp
from jax import lax
from jax.experimental import pallas as pl
from jax.experimental.pallas import tpu as pltpu
from jax.sharding import PartitionSpec as P

MESH = pl.DeviceIdType.MESH
F32 = jnp.float32
BF16 = jnp.bfloat16


def kernel(
    n_row, n_col, vb,
    blocks, columns, vectors,
    out0, out1, out2, out3,
    perm_v, keep_v, last_v, perm, keep, last, gcol,
    w, wt, cv0, cv1, cv2, cv3, pb, rb, rv, tb0, tb1, seg, sb, sib, hb, rr,
    load_sem, order_sem, ag_send, ag_recv, fw_send, fw_recv, sc_send, sc_recv,
    gc_send, gc_recv, sx_send, sx_recv, sr_send, sr_recv,
):
    row = lax.axis_index("row")
    col = lax.axis_index("col")
    chips = n_row // 2
    nx, nz = chips // 2, n_col // 2
    chip, core = row // 2, row % 2
    x, y = chip // 2, chip % 2
    h, z = col // nz, col % nz
    rows = n_col * vb
    nnz = w.shape[0] // rows
    slots = rows * nnz
    cols = n_row * vb
    k2, bs = vectors.shape[1] // 2, vectors.shape[2]
    sibling = {"row": chip * 2 + 1 - core}

    def chip_to(e):
        return ((x + e % nx) % nx) * 2 + (y + e // nx) % 2

    def chip_from(e):
        return ((x + nx - e % nx) % nx) * 2 + (y + e // nx) % 2

    def col_to(e):
        return ((h + e // nz) % 2) * nz + (z + e % nz) % nz

    def col_from(e):
        return ((h + e // nz) % 2) * nz + (z + nz - e % nz) % nz

    def hops(e, ring, across):
        return min(e % ring, ring - e % ring) + across * (e // ring)

    far_chips = sorted(range(1, chips), key=lambda e: -hops(e, nx, 1))
    far_cols = sorted(range(1, n_col), key=lambda e: -hops(e, nz, 2))

    def each_chip(step):
        for e in far_chips:
            step(e)

    def each_col(step):
        for e in far_cols:
            step(e)

    def load(d):
        part = pl.ds(d * vb * nnz, vb * nnz)
        return pltpu.make_async_copy(blocks.at[part], w.at[part], load_sem.at[d])

    for d in range(n_col):
        load(d).start()

    barrier = pltpu.get_barrier_semaphore()
    pl.semaphore_signal(barrier, inc=1, device_id=sibling, device_id_type=MESH)

    def greet_chip(e):
        pl.semaphore_signal(barrier, inc=1, device_id={"row": chip_to(e) * 2 + core}, device_id_type=MESH)

    def greet_col(e):
        pl.semaphore_signal(barrier, inc=1, device_id={"col": col_to(e)}, device_id_type=MESH)

    each_chip(greet_chip)
    each_col(greet_col)

    zero = jnp.zeros((k2, bs), F32)
    seg[slots] = zero.astype(BF16)

    class Part:
        def __init__(self, rnd, half):
            self.at = rnd * 2 + half
            self.mine = pl.ds(half * k2, k2)
            self.image = out0 if rnd == 0 else out2
            self.back = out1 if rnd == 0 else out3
            self.cv = (cv0, cv1, cv2, cv3)[self.at]
            self.tb = (tb0, tb1)[half]
            self.pb, self.rb, self.rv = pb.at[self.at], rb.at[self.at], rv.at[self.at]
            self.sb, self.sib = sb.at[self.at], sib.at[self.at]
            self.hb, self.rr = hb.at[self.at], rr.at[self.at]

        def shard(self, r):
            return self.cv.at[pl.ds(r * vb, vb)]

        def copy(self, src, dst, send, recv, j, to):
            return pltpu.make_async_remote_copy(
                src_ref=src, dst_ref=dst, send_sem=send.at[self.at, j], recv_sem=recv.at[self.at, j],
                device_id=to, device_id_type=MESH)

        def gather(self, e, owner=None):
            at = self.shard(row if owner is None else owner)
            return self.copy(at, at, ag_send, ag_recv, e, {"row": chip_to(e) * 2 + core})

        def forwarding(self, e, owner):
            at = self.shard(owner)
            return self.copy(at, at, fw_send, fw_recv, e, sibling)

        def gather_start(self):
            self.cv[cols] = zero.astype(BF16)
            each_chip(lambda e: self.gather(e).start())
            self.forwarding(0, row).start()

        def pass_on(self, first, end):
            def one(e, c):
                owner = chip_from(e) * 2 + core
                self.gather(e, owner).wait_recv()
                self.forwarding(e, owner).start()
                return c
            lax.fori_loop(first, end, one, 0)

        def gather_end(self):
            def one(e, c):
                self.forwarding(e, chip_from(e) * 2 + 1 - core).wait_recv()
                return c
            lax.fori_loop(0, chips, one, 0)

        def partial(self, d):
            done = []
            for i in range(vb):
                base = (d * vb + i) * nnz
                v = jnp.concatenate([self.cv[gcol[0, base + q]] for q in range(nnz)], axis=1)
                m = wt[pl.ds(base, nnz)].reshape(nnz * bs, bs)
                done.append(jnp.dot(v, m, preferred_element_type=F32).astype(BF16))
            for i in range(vb):
                self.pb[d, i] = done[i]

        def scatter(self, e):
            return self.copy(self.pb.at[col_to(e)], self.rb.at[e], sc_send, sc_recv, e, {"col": col_to(e)})

        def forward(self, first, end):
            def one(s, c):
                e = n_col - 1 - s
                self.partial(col_to(e))

                @pl.when(e > 0)
                def _():
                    self.scatter(e).start()
                return c
            lax.fori_loop(first, end, one, 0)

        def reduce_rows(self):
            each_col(lambda e: self.scatter(e).wait_recv())
            total = self.pb[col].astype(F32)
            for e in range(1, n_col):
                total += self.rb[e].astype(F32)
            total = total.astype(BF16)
            self.rv[pl.ds(col * vb, vb)] = total
            each_col(lambda e: self.spread(e).start())
            self.image[:, self.mine] = total

        def spread(self, e, owner=None):
            at = self.rv.at[pl.ds((col if owner is None else owner) * vb, vb)]
            return self.copy(at, at, gc_send, gc_recv, e, {"col": col_to(e)})

        def terms(self, first, end):
            def one(e, c):
                d = col_from(e)

                @pl.when(e > 0)
                def _():
                    self.spread(e, d).wait_recv()
                for i in range(vb):
                    at = d * vb + i
                    v = self.rv[at]
                    done = []
                    for q in range(0, nnz, 2):
                        base = at * nnz + q
                        m = jnp.concatenate([w[base], w[base + 1]], axis=1)
                        r = jnp.dot(v, m, preferred_element_type=F32)
                        done += [r[:, :bs], r[:, bs:]]
                    for q in range(nnz):
                        self.tb[at * nnz + q] = done[q]
                return c
            lax.fori_loop(first, end, one, 0)

        def column_chunk(self, r):
            ends = [seg[last[0, r * vb + i]] for i in range(vb)]
            for i in range(vb):
                self.sb[r, i] = ends[i]

        def swap(self, q):
            return self.copy(self.sb.at[q * 2 + 1 - core], self.sib.at[q], sx_send, sx_recv, q, sibling)

        def combine(self):
            def running(u, total):
                read = [self.tb[perm[0, u * 16 + q]] for q in range(16)]
                sums = []
                for first in range(0, 16, 4):
                    chain, value = None, None
                    for q in range(first, first + 4):
                        stay = keep[0, u * 16 + q]
                        chain = stay if q == first else chain * stay
                        value = read[q] if q == first else value * stay + read[q]
                        sums.append(total * chain + value)
                    total = sums[-1]
                for q in range(16):
                    seg[u * 16 + q] = sums[q].astype(BF16)
                return total

            lax.fori_loop(0, slots // 16, running, zero)

            def theirs(s, c):
                q = chip_to(chips - 1 - s)
                self.column_chunk(q * 2 + 1 - core)
                self.swap(q).start()
                return c

            def ours(r, c):
                self.column_chunk(r * 2 + core)
                return c

            lax.fori_loop(0, chips, theirs, 0)
            lax.fori_loop(0, chips, ours, 0)

        def scatter_row(self, e):
            return self.copy(self.hb.at[e], self.rr.at[e], sr_send, sr_recv, e, {"row": chip_to(e) * 2 + core})

        def pair(self):
            def one(e):
                q = chip_to(e)
                self.swap(q).wait_recv()
                self.hb[e] = (self.sb[q * 2 + core].astype(F32) + self.sib[q].astype(F32)).astype(BF16)
                self.scatter_row(e).start()
            each_chip(one)
            self.swap(chip).wait_recv()

        def reduce_cols(self, following):
            each_chip(lambda e: self.scatter_row(e).wait_recv())
            total = self.sb[row].astype(F32) + self.sib[chip].astype(F32)
            for e in range(1, chips):
                total += self.rr[e].astype(F32)
            total = total.astype(BF16)
            if following is not None:
                following.cv[pl.ds(row * vb, vb)] = total
                following.gather_start()
            self.back[:, self.mine] = total

        def end(self):
            def by_chip(e):
                self.gather(e).wait_send()
                self.forwarding(e, row).wait_send()
                self.scatter_row(e).wait_send()
                self.swap(e).wait_send()

            def by_col(e):
                self.scatter(e).wait_send()
                self.spread(e).wait_send()

            each_chip(by_chip)
            each_col(by_col)
            self.forwarding(0, row).wait_send()
            self.swap(0).wait_send()

    parts = [[Part(rnd, half) for half in range(2)] for rnd in range(2)]
    a, b = parts[0]
    for part in (a, b):
        for i in range(vb):
            part.cv[row * vb + i] = vectors[i, part.mine]
    pl.semaphore_wait(barrier, 1 + (chips - 1) + (n_col - 1))
    a.gather_start()
    b.gather_start()

    def turn(d, c):
        load(d).wait()

        def one(i, cc):
            wt[d * vb * nnz + i] = w[d * vb * nnz + i].T
            return cc
        lax.fori_loop(0, vb * nnz, one, 0, unroll=8)
        return c

    moves = [
        pltpu.make_async_copy(src, dst, order_sem.at[j])
        for j, (src, dst) in enumerate(((columns, gcol), (perm_v, perm), (keep_v, keep), (last_v, last)))
    ]
    moves[0].start()
    early = n_col - n_col // 4
    lax.fori_loop(0, early, turn, 0)
    a.pass_on(1, chips)
    lax.fori_loop(early, n_col, turn, 0)

    moves[0].wait()
    near, half = (chips + 1) // 2, n_col // 2
    for rnd in range(2):
        a, b = parts[rnd]
        a.gather_end()
        cut = n_col - n_col // 4 if rnd == 0 else n_col
        a.forward(0, cut)
        b.pass_on(1, chips)
        a.forward(cut, n_col)
        b.gather_end()
        b.forward(0, n_col)
        a.reduce_rows()
        a.terms(0, 1)
        if rnd == 0:
            column_order(columns, nnz, cols, perm_v, keep_v, last_v)
            for move in moves[1:]:
                move.start()
        else:
            for part in parts[0]:
                part.end()
        b.reduce_rows()
        if rnd == 0:
            for move in moves[1:]:
                move.wait()
        b.terms(0, 1)
        a.terms(1, n_col)
        a.combine()
        b.terms(1, half)
        a.pair()
        b.terms(half, n_col)
        b.combine()
        b.pair()
        if rnd == 0:
            a.reduce_cols(parts[1][0])
            parts[1][0].pass_on(1, near)
            b.reduce_cols(parts[1][1])
            parts[1][0].pass_on(near, chips)
        else:
            a.end()
            a.reduce_cols(None)
            b.end()
            b.reduce_cols(None)


def copy_out(*refs):
    n = len(refs) // 2
    for j in range(n):
        refs[n + j][...] = refs[j][...]


def column_order(columns, nnz, col_count, perm, keep, last):
    slots = columns.shape[1]
    rows = slots // nnz
    ts = lax.broadcasted_iota(jnp.int32, (rows, slots), 1)
    block_row = lax.broadcasted_iota(jnp.int32, (rows, slots), 0)
    parts = [
        jnp.sum(jnp.where(block_row * nnz + q == ts, columns[...], 0), axis=1, keepdims=True)
        for q in range(nnz)
    ]
    js = lax.broadcasted_iota(jnp.int32, (rows, col_count), 1)
    ones = jnp.concatenate([(part == js).astype(jnp.int32) for part in parts], axis=0)
    below = sum(jnp.sum((part < js).astype(jnp.int32), axis=0, keepdims=True) for part in parts)
    upto = ones
    step = 1
    while step < slots:
        upto = upto + jnp.concatenate([jnp.zeros((step, col_count), jnp.int32), upto[:slots - step]], axis=0)
        step *= 2
    held = upto[slots - 1:]
    last[...] = jnp.where(held > 0, below + held - 1, slots)
    found, follows = 0, 0
    for q, part in enumerate(parts):
        at = slice(q * rows, (q + 1) * rows)
        before = jnp.sum(ones[at] * (upto[at] - 1), axis=1, keepdims=True)
        rank = before + jnp.sum(ones[at] * below, axis=1, keepdims=True)
        rank = jnp.where(part < col_count, rank, slots)
        slot = block_row * nnz + q
        hit = rank == ts
        found += jnp.sum(jnp.where(hit, slot, 0), axis=0, keepdims=True)
        follows += jnp.sum(jnp.where(hit & (before > 0), 1, 0), axis=0, keepdims=True)
    perm[...] = found
    keep[...] = follows.astype(F32)


def body(n_row, n_col, blocks, columns, counts, vectors):
    rows, nnz, bs, _ = blocks.shape
    vb, k, _ = vectors.shape
    k2 = k // 2
    slots = rows * nnz
    cols = n_row * vb
    chips = n_row // 2
    active = jnp.arange(nnz, dtype=jnp.int32)[None, :] < counts
    gcol = jnp.where(active, columns, cols).astype(jnp.int32).reshape(1, slots)
    any_space = pl.BlockSpec(memory_space=pl.ANY)
    vmem = pl.BlockSpec(memory_space=pltpu.VMEM)
    dma = pltpu.SemaphoreType.DMA
    order = [((1, slots), jnp.int32), ((1, slots), F32), ((1, cols), jnp.int32)]
    result = [jax.ShapeDtypeStruct((vb, k, bs), BF16)] * 4
    outs = pl.pallas_call(
        functools.partial(kernel, n_row, n_col, vb),
        out_shape=result,
        in_specs=[any_space, vmem, vmem],
        out_specs=[vmem] * 4,
        scratch_shapes=[
            *[space(shape, kind) for space in (pltpu.VMEM, pltpu.SMEM) for shape, kind in order],
            pltpu.SMEM((1, slots), jnp.int32),
            pltpu.VMEM((slots, bs, bs), BF16),
            pltpu.VMEM((slots, bs, bs), BF16),
            *[pltpu.VMEM((cols + 1, k2, bs), BF16)] * 4,
            pltpu.VMEM((4, n_col, vb, k2, bs), BF16),
            pltpu.VMEM((4, n_col, vb, k2, bs), BF16),
            pltpu.VMEM((4, rows, k2, bs), BF16),
            *[pltpu.VMEM((slots, k2, bs), F32)] * 2,
            pltpu.VMEM((slots + 1, k2, bs), BF16),
            pltpu.VMEM((4, n_row, vb, k2, bs), BF16),
            pltpu.VMEM((4, chips, vb, k2, bs), BF16),
            pltpu.VMEM((4, chips, vb, k2, bs), BF16),
            pltpu.VMEM((4, chips, vb, k2, bs), BF16),
            dma((n_col,)), dma((4,)),
            dma((4, chips)), dma((4, chips)),
            dma((4, chips)), dma((4, chips)),
            dma((4, n_col)), dma((4, n_col)),
            dma((4, n_col)), dma((4, n_col)),
            dma((4, chips)), dma((4, chips)),
            dma((4, chips)), dma((4, chips)),
        ],
        compiler_params=pltpu.CompilerParams(
            collective_id=0, has_side_effects=True, vmem_limit_bytes=58 << 20),
        name="krylov",
    )(blocks.reshape(slots, bs, bs), gcol, vectors)
    outs = pl.pallas_call(
        copy_out,
        out_shape=result,
        in_specs=[vmem] * 4,
        out_specs=[vmem] * 4,
        name="results",
    )(*outs)
    return tuple(outs)


def solution(mesh):
    in_specs = (
        P("row", "col", None, None),
        P("row", "col"),
        P("row", "col"),
        P(("col", "row"), None, None),
    )
    out_specs = (
        P(("row", "col"), None, None),
        P(("col", "row"), None, None),
        P(("row", "col"), None, None),
        P(("col", "row"), None, None),
    )
    run = functools.partial(body, mesh.shape["row"], mesh.shape["col"])
    return jax.shard_map(run, mesh=mesh, in_specs=in_specs, out_specs=out_specs, check_vma=False)
```
